32 devices in a mesh: ctx: 4 (over y, core), exp: 8 (over z, x).
Axes of the slice: x: 2, y: 2, z: 4, core: 2. Of those that a mesh axis runs over, the one named last changes fastest.
Arguments:
- mixer_input: bfloat16 [512, 2, 8192], P('ctx', None, 'exp'), may hold values from -6 to 6
- gate_in: bfloat16 [512, 2, 8192], P('ctx', None, 'exp'), may hold values from -6 to 6
- step_size: float32 [512, 2, 8192], P('ctx', None, 'exp'), may hold values from 0.004 to 10
- decay_rate: float32 [16, 8192], P(None, 'exp'), may hold values from 0.03 to 2.5
- state_in: float32 [512, 2, 16], P('ctx'), may hold values from -6 to 6
- state_out: float32 [512, 2, 16], P('ctx'), may hold values from -6 to 6
- skip: float32 [8192], P('exp'), may hold values from 0.5 to 1.5
- out_proj: bfloat16 [8192, 4096], P('exp', 'ctx'), may hold values from -0.0625 to 0.0625
- hidden_in: bfloat16 [512, 2, 4096], P('ctx', None, 'exp'), may hold values from -14 to 14
- norm_gain: float32 [4096], replicated, may hold values from 0.4 to 2.5
- w_gate: bfloat16 [8, 4096, 7168], P('exp', None, 'ctx'), may hold values from -0.09375 to 0.09375
- w_up: bfloat16 [8, 4096, 7168], P('exp', None, 'ctx'), may hold values from -0.09375 to 0.09375
- w_down: bfloat16 [8, 7168, 4096], P('exp', 'ctx'), may hold values from -0.0625 to 0.0625
- route_ids: int32 [512, 2, 2], P('ctx'), may hold values from 0 to 7, all different within a row; in each aligned block of 256 rows (0 to 255, 256 to 511, ..., all dimensions but the last counted through in order) at most 128 rows name the same one
- route_weight: float32 [512, 2, 2], P('ctx'), may hold values from 0.1 to 0.9
Outputs:
- layer_out: bfloat16 [512, 2, 4096], P('ctx', None, 'exp')
The draws below stay inside these ranges and needn't reach their ends.
Inputs may be any that keep to these rules, and one draw needn't show every extreme that they name: `route_ids`: the 2 experts of a token differ; within the rows of one index of ctx no expert is named by more than 128 rows.
All inputs are finite; a program needn't handle non-finite values.
Results may differ from the reference program's by a relative error of at most 0.009.
Values may be sent and summed in bfloat16 or wider, within the bound.
A program may use at most 256 MiB of HBM per device.

```python
import math
import jax
import jax.numpy as jnp
import numpy as np
from jax import lax

D = 4096
STATE = 16
TOP = 2
INNER = 8192
HID = 7168
BATCH = 2
EXPERTS = 8
TOK_DEV = 256
LEN = 512
CAP = 128
N_CTX = 4


def draw_step_size(key, part):
    key_base, key_where, key_height = jax.random.split(key, 3)
    shape = (LEN, BATCH, INNER)
    baseline = 0.01 * jnp.exp(jax.random.uniform(key_base, shape, jnp.float32, -0.7, 0.7))
    spots = jax.random.randint(key_where, (2, BATCH), 0, LEN)
    places = jnp.arange(LEN)[:, None]
    bursting = jnp.any(places[None, :, :] == spots[:, None, :], axis=0)
    heights = jnp.exp(jax.random.uniform(key_height, shape, jnp.float32, math.log(5.0), math.log(10.0)))
    return jnp.where(bursting[:, :, None], heights, baseline)


def draw_decay_rate(key, part):
    shape = (STATE, INNER)
    expo = jax.random.uniform(key, shape, jnp.float32, math.log(0.03), math.log(2.5))
    return jnp.exp(expo)


def draw_hidden_in(key, part):
    key_value, key_rough = jax.random.split(jax.random.fold_in(key, 7), 2)
    shape = (LEN, BATCH, D)
    place = jnp.arange(D, dtype=jnp.float32) / max(D - 1, 1)
    rough = jnp.exp(jax.random.uniform(key_rough, (D,), jnp.float32, math.log(0.7), math.log(1.4)))
    profile = jnp.exp(math.log(0.3) + (math.log(3.0) - math.log(0.3)) * place) * rough
    values = jnp.clip(jax.random.normal(key_value, shape, jnp.float32), -3.0, 3.0)
    return (values * profile).astype(jnp.bfloat16)


def shard_levels(rng, shape, cuts, smallest, largest):
    loudness = 1.0
    for axis_at, parts in cuts:
        draws = jax.random.uniform(jax.random.fold_in(jax.random.fold_in(rng, 6), axis_at), (parts,), jnp.float32, smallest / len(cuts), largest / len(cuts))
        loudness = loudness * jnp.repeat(jnp.exp(draws), shape[axis_at] // parts).reshape((-1,) + (1,) * (len(shape) - 1 - axis_at))
    return loudness


def deal_out(own_key, own, number, rows, number_of, top, bound, slope):
    ranking = jax.random.permutation(own_key, number_of)
    packed, common = shares(number_of, rows * top, bound, slope, True), shares(number_of, rows * top, bound, slope, False)
    places = jnp.arange(number_of)

    def named(sizes, offset_by):
        used = int((sizes > 0).sum())
        fixed = max(1, used // 4)
        passed = fixed + (places - fixed + offset_by * (used - fixed)) % max(1, number_of - fixed)
        return jnp.zeros((number_of,), jnp.int32).at[ranking[jnp.where(places < fixed, places, passed)]].set(jnp.asarray(sizes, jnp.int32))

    sizes = jnp.where(number % 4 == 0, named(packed, number // 4), named(common, number - number // 4 - 1))
    mixed = jax.random.permutation(jax.random.fold_in(own, 3), number_of)
    donor, receiver = mixed[0:number_of // 2 * 2:2], mixed[1:number_of // 2 * 2:2]
    room = jnp.minimum(sizes[donor] - 1, bound - sizes[receiver]) // 2
    room = jnp.where((donor == ranking[0]) | (receiver == ranking[0]) | (sizes[receiver] == 0), 0, jnp.maximum(room, 0))
    passed = jax.random.randint(jax.random.fold_in(own, 4), (number_of // 2,), 0, 1 << 20) % (room + 1)
    sizes = sizes.at[donor].add(-passed).at[receiver].add(passed)
    items = jnp.searchsorted(jnp.cumsum(sizes), jnp.arange(rows * top), side="right").astype(jnp.int32)
    listing = items.reshape(top, rows).T
    listing = listing[jax.random.permutation(jax.random.fold_in(own, 1), rows)]
    offset_by = jax.random.randint(jax.random.fold_in(own, 2), (rows, 1), 0, top)
    return jnp.take_along_axis(listing, (jnp.arange(top)[None, :] + offset_by) % top, axis=1)


def shares(amount, total, most, skew, full):
    weights = [(1 << 20) // math.isqrt(grade ** skew) + 1 for grade in range(1, amount + 1)]
    largest = most if full else min(most, max(-(-total // amount), total * weights[0] // sum(weights)))
    least = 1 if total - largest >= amount - 1 else 0
    holding, spare = [largest] + [least] * (amount - 1), total - largest - least * (amount - 1)
    while spare > 0:
        candidates = [i for i in range(1, amount) if holding[i] < largest] or [i for i in range(1, amount) if holding[i] < most]
        mass, budget = sum([weights[i] for i in candidates]), spare
        for i in candidates:
            more = min(most - holding[i], max(1, budget * weights[i] // mass), spare)
            holding[i] = holding[i] + more
            spare = spare - more
    return np.array(holding)


def scatter_about(rng, extent, spread, limit, pieces=(), held_as=jnp.bfloat16):
    level = shard_levels(rng, extent, pieces, -0.22, 0.18) if pieces else 1.0
    values = jax.random.normal(rng, extent, jnp.float32) * spread * level
    return jnp.minimum(jnp.maximum(values, -limit), limit).astype(held_as)


def setup_inputs(seed: int = 0) -> dict:
    streams_of = jax.random.split(jax.random.key(seed), 16)
    mixer_input = scatter_about(streams_of[0], (LEN, BATCH, INNER), 1.0, 6.0, ((0, 4), (2, 8)))
    gate_in = scatter_about(streams_of[1], (LEN, BATCH, INNER), 1.0, 6.0, ((0, 4), (2, 8)))
    step_size = draw_step_size(jax.random.fold_in(streams_of[15], 71), 0)
    decay_rate = draw_decay_rate(jax.random.fold_in(streams_of[15], 71), 0)
    state_in = scatter_about(streams_of[4], (LEN, BATCH, STATE), 1.0, 6.0, ((0, 4),), jnp.float32)
    state_out = scatter_about(streams_of[5], (LEN, BATCH, STATE), 1.0, 6.0, ((0, 4),), jnp.float32)
    skip = jnp.clip(0.5 + 1.0 * jax.random.uniform(streams_of[6], (INNER,), jnp.float32) ** shard_levels(streams_of[6], (INNER,), ((0, 8),), -0.2, 0.2), 0.5, 1.5)
    out_proj = scatter_about(streams_of[7], (INNER, D), INNER ** -0.5, 0.0625, ((0, 8), (1, 4)))
    hidden_in = draw_hidden_in(jax.random.fold_in(streams_of[15], 71), 0)
    norm_gain = jnp.clip(jnp.exp(jax.random.uniform(streams_of[9], (D,), jnp.float32, math.log(0.4), math.log(2.5))), 0.4, 2.5)
    w_gate = scatter_about(streams_of[10], (EXPERTS, D, HID), D ** -0.5, 0.09375, ((0, 8), (2, 4)))
    w_up = scatter_about(streams_of[11], (EXPERTS, D, HID), D ** -0.5, 0.09375, ((0, 8), (2, 4)))
    w_down = scatter_about(streams_of[12], (EXPERTS, HID, D), HID ** -0.5, 0.0625, ((0, 8), (1, 4)))
    route_ids_keys = jax.random.split(jax.random.fold_in(streams_of[13], 1), LEN * BATCH // TOK_DEV)
    route_ids_turns = jax.random.permutation(jax.random.fold_in(streams_of[13], 3), LEN * BATCH // TOK_DEV)
    route_ids = jax.vmap(lambda own, number: deal_out(jax.random.fold_in(streams_of[13], 2), own, number, TOK_DEV, EXPERTS, TOP, CAP, 2))(route_ids_keys, route_ids_turns).reshape((LEN, BATCH, TOP))
    route_weight = jnp.clip(0.1 + 0.79999997 * jax.random.uniform(streams_of[14], (LEN, BATCH, TOP), jnp.float32) ** shard_levels(streams_of[14], (LEN, BATCH, TOP), ((0, 4),), -0.2, 0.2), 0.1, 0.9)
    return dict(mixer_input=mixer_input, gate_in=gate_in, step_size=step_size, decay_rate=decay_rate, state_in=state_in, state_out=state_out, skip=skip, out_proj=out_proj, hidden_in=hidden_in, norm_gain=norm_gain, w_gate=w_gate, w_up=w_up, w_down=w_down, route_ids=route_ids, route_weight=route_weight)


epsilon = 1e-06

def reference(mixer_input, gate_in, step_size, decay_rate, state_in, state_out, skip, out_proj, hidden_in, norm_gain, w_gate, w_up, w_down, route_ids, route_weight):
    signal = mixer_input.astype(jnp.float32)

    def advance(carried, inputs):
        sig_now, step_now, into_now, outof_now = inputs
        factor = jnp.exp(-step_now[:, None, :] * decay_rate[None, :, :])
        carried = factor * carried + (step_now * sig_now)[:, None, :] * into_now[:, :, None]
        return (carried, lax.optimization_barrier(jnp.sum(outof_now[:, :, None] * carried, axis=1)))
    start_state = jnp.zeros((BATCH, STATE, INNER), jnp.float32)
    _, scanned = lax.scan(advance, start_state, (signal, step_size, state_in, state_out))
    mixed = ((scanned + skip * signal) * jax.nn.silu(gate_in.astype(jnp.float32))).astype(jnp.bfloat16)
    all_rows = LEN * BATCH
    mixer_proj = jnp.dot(mixed.reshape(all_rows, INNER), out_proj, preferred_element_type=jnp.float32)
    residual = hidden_in.reshape(all_rows, D).astype(jnp.float32) + mixer_proj
    scale_rows = lax.rsqrt(lax.optimization_barrier(jnp.mean(residual * residual, axis=1)) + epsilon)
    normed = (residual * scale_rows[:, None] * norm_gain).astype(jnp.bfloat16)
    routed = route_ids.reshape(all_rows, TOP)
    weights = route_weight.reshape(all_rows, TOP)
    group = HID // N_CTX
    total_slots = N_CTX * CAP
    row_ids = jnp.arange(all_rows, dtype=jnp.int32)
    block_ids = row_ids // TOK_DEV

    def expert_term(expert, accum):
        matches = routed == expert
        chosen = jnp.any(matches, axis=1)
        strength = lax.optimization_barrier(jnp.sum(jnp.where(matches, weights, 0.0), axis=1))
        position = jnp.cumsum(chosen.astype(jnp.int32).reshape(N_CTX, TOK_DEV), axis=1).reshape(all_rows) - 1
        slot_of = jnp.where(chosen, block_ids * CAP + position, total_slots).astype(jnp.int32)
        slot_token = jnp.zeros((total_slots,), jnp.int32).at[slot_of].set(row_ids, mode='drop')
        filled = jnp.zeros((total_slots,), jnp.bool_).at[slot_of].set(True, mode='drop')
        gathered = jnp.where(filled[:, None], normed[slot_token], jnp.zeros((), jnp.bfloat16)).astype(jnp.bfloat16)
        gate_part = jnp.dot(gathered, w_gate[expert], preferred_element_type=jnp.float32)
        up_part = jnp.dot(gathered, w_up[expert], preferred_element_type=jnp.float32)
        activ = (jax.nn.silu(gate_part) * up_part).astype(jnp.bfloat16)
        down_all = w_down[expert]
        returned = jnp.zeros((total_slots, D), jnp.float32)
        for grp in range(N_CTX):
            partial_value = jnp.dot(activ[:, grp * group:(grp + 1) * group], down_all[grp * group:(grp + 1) * group], preferred_element_type=jnp.float32).astype(jnp.bfloat16)
            partial_value = lax.optimization_barrier(partial_value)
            returned = returned + partial_value.astype(jnp.float32)
        picked = returned[jnp.clip(slot_of, 0, total_slots - 1)]
        return accum + jnp.where(chosen, strength, 0.0)[:, None] * picked
    experts_sum = lax.fori_loop(0, EXPERTS, expert_term, jnp.zeros((all_rows, D), jnp.float32))
    return (residual + experts_sum).astype(jnp.bfloat16).reshape(LEN, BATCH, D)
```

```python
import functools
import math

import jax
import jax.numpy as jnp
from jax import lax
from jax.experimental import pallas as pl
from jax.experimental.pallas import tpu as pltpu
from jax.sharding import PartitionSpec as P

epsilon = 1e-06
f32, bf16 = jnp.float32, jnp.bfloat16
MESH = pl.DeviceIdType.MESH
VMEM_LIMIT = 48 * 1024 * 1024
HBM = pl.BlockSpec(memory_space=pl.ANY)
SMEM = pl.BlockSpec(memory_space=pltpu.SMEM)
LOCAL = pl.BlockSpec(memory_space=pltpu.VMEM)


def factors(count):
    inner = 2 ** (count.bit_length() // 2 - (1 if count.bit_length() % 2 == 0 else 0))
    return count // inner, inner


def ends_kernel(length, prompts, states, step_ref, signal_ref, rate_ref, into_ref, end_ref):
    tile = step_ref.shape[1:]
    for b in range(prompts):

        def chunk(i, carry):
            held, total = carry
            for u in range(4):
                row = (i * 4 + u) * prompts + b
                step = step_ref[row]
                inflow = step * signal_ref[row]
                held = tuple(
                    jnp.exp2(step * rate_ref[n]) * held[n] + inflow * into_ref[row * states + n]
                    for n in range(states)
                )
                total = total + step
            return held, total

        zero = jnp.zeros(tile, f32)
        held, total = lax.fori_loop(0, length // 4, chunk, ((zero,) * states, zero))
        for n in range(states):
            end_ref[b, n] = held[n]
        end_ref[b, states] = total


def scan_kernel(
    length, prompts, states, step_ref, signal_ref, rate_ref, into_ref, outof_ref, enter_ref, out_ref
):
    for b in range(prompts):

        def chunk(i, held):
            for u in range(4):
                row = (i * 4 + u) * prompts + b
                step = step_ref[row]
                inflow = step * signal_ref[row]
                held = tuple(
                    jnp.exp2(step * rate_ref[n]) * held[n] + inflow * into_ref[row * states + n]
                    for n in range(states)
                )
                terms = [held[n] * outof_ref[row * states + n] for n in range(states)]
                while len(terms) > 1:
                    terms = [p + q for p, q in zip(terms[::2], terms[1::2])]
                out_ref[row] = terms[0]
            return held

        lax.fori_loop(0, length // 4, chunk, tuple(enter_ref[b, n] for n in range(states)))


def exchange(x, out_shape, axis, count, member, mine, source, target, ident):
    def kernel(x_ref, o_ref, send_sem, recv_sem, local_sem):
        q = mine(lax.axis_index(axis))
        me = lax.axis_index(axis)
        barrier = pltpu.get_barrier_semaphore()
        for k in range(1, count):
            peer = member(me, lax.rem(q + k, count))
            pl.semaphore_signal(barrier, inc=1, device_id={axis: peer}, device_id_type=MESH)
        pl.semaphore_wait(barrier, count - 1)
        copies = []
        for k in range(1, count):
            r = lax.rem(q + k, count)
            copies.append(
                pltpu.make_async_remote_copy(
                    src_ref=source(x_ref, r),
                    dst_ref=target(o_ref, q),
                    send_sem=send_sem.at[k - 1],
                    recv_sem=recv_sem.at[k - 1],
                    device_id={axis: member(me, r)},
                    device_id_type=MESH,
                )
            )
            copies[-1].start()
        own = pltpu.make_async_copy(source(x_ref, q), target(o_ref, q), local_sem)
        own.start()
        own.wait()
        for copy in copies:
            copy.wait()

    return pl.pallas_call(
        kernel,
        out_shape=jax.ShapeDtypeStruct(out_shape, x.dtype),
        in_specs=[HBM],
        out_specs=HBM,
        scratch_shapes=[
            pltpu.SemaphoreType.DMA((count - 1,)),
            pltpu.SemaphoreType.DMA((count - 1,)),
            pltpu.SemaphoreType.DMA,
        ],
        compiler_params=pltpu.CompilerParams(collective_id=ident, has_side_effects=True),
    )(x)


def gather_ctx(x, out_shape, count, target, ident):
    axis, chips = "ctx", count // 2

    def kernel(x_ref, o_ref, send_sem, recv_sem, local_sem):
        me = lax.axis_index(axis)
        chip, core = me // 2, lax.rem(me, 2)
        twin = chip * 2 + (1 - core)
        barrier = pltpu.get_barrier_semaphore()
        partners = [twin] + [lax.rem(chip + k, chips) * 2 + core for k in range(1, chips)]
        for peer in partners:
            pl.semaphore_signal(barrier, inc=1, device_id={axis: peer}, device_id_type=MESH)
        pl.semaphore_wait(barrier, chips)

        def push(src, owner, slot, peer):
            copy = pltpu.make_async_remote_copy(
                src_ref=src,
                dst_ref=target(o_ref, owner),
                send_sem=send_sem.at[slot],
                recv_sem=recv_sem.at[slot],
                device_id={axis: peer},
                device_id_type=MESH,
            )
            copy.start()
            return copy

        across = [push(x_ref, me, k, partners[k]) for k in range(1, chips)]
        pending = [push(x_ref, me, 0, twin)]
        own = pltpu.make_async_copy(x_ref, target(o_ref, me), local_sem)
        own.start()
        for k in range(1, chips):
            across[k - 1].wait_recv()
            owner = lax.rem(chip + chips - k, chips) * 2 + core
            pending.append(push(target(o_ref, owner), owner, chips - 1 + k, twin))
        own.wait()
        for copy in across:
            copy.wait_send()
        for copy in pending:
            copy.wait()

    slots = 2 * chips - 1
    return pl.pallas_call(
        kernel,
        out_shape=jax.ShapeDtypeStruct(out_shape, x.dtype),
        in_specs=[HBM],
        out_specs=HBM,
        scratch_shapes=[
            pltpu.SemaphoreType.DMA((slots,)),
            pltpu.SemaphoreType.DMA((slots,)),
            pltpu.SemaphoreType.DMA,
        ],
        compiler_params=pltpu.CompilerParams(collective_id=ident, has_side_effects=True),
    )(x)


def block(ref, r):
    return ref.at[r]


def scatter_sum(x, axis, count, ident):
    outer, inner = factors(count) if axis == "exp" else (count // 2, 2)
    rows, columns = x.shape[1:]
    x = x.reshape(outer, inner, rows, columns).transpose(1, 0, 2, 3)
    got = exchange(
        x, x.shape, axis, inner,
        lambda me, r: me // inner * inner + r, lambda me: lax.rem(me, inner),
        block, block, ident,
    )
    part = jnp.sum(got.astype(f32), axis=0).astype(bf16)
    got = exchange(
        part, part.shape, axis, outer,
        lambda me, r: r * inner + lax.rem(me, inner), lambda me: me // inner,
        block, block, ident + 1,
    )
    return jnp.sum(got.astype(f32), axis=0)


def on_device(
    mixer_input,
    gate_in,
    step_size,
    decay_rate,
    state_in,
    state_out,
    skip,
    out_proj,
    hidden_in,
    norm_gain,
    w_gate,
    w_up,
    w_down,
    route_ids,
    route_weight,
):
    slab_len, prompts, channels = mixer_input.shape
    states = decay_rate.shape[0]
    tokens = slab_len * prompts
    n_ctx, n_exp = lax.axis_size("ctx"), lax.axis_size("exp")
    ctx, exp = lax.axis_index("ctx"), lax.axis_index("exp")
    share = hidden_in.shape[-1]
    halves = n_exp // n_ctx
    cap = 4 * tokens // (w_gate.shape[0] * n_exp)

    swap = [
        (c * n_exp + e, (e // halves) * n_exp + c * halves + e % halves)
        for c in range(n_ctx)
        for e in range(n_exp)
    ]
    hidden = lax.ppermute(hidden_in.reshape(tokens, share), ("ctx", "exp"), swap)
    routes = lax.all_gather(route_ids.reshape(tokens, -1), "ctx", axis=0)
    slab = exp // halves

    def selector(routed):
        named = jnp.any(routed[:, :, None] == jnp.arange(n_exp)[None, None, :], axis=1)
        place = jnp.cumsum(named.astype(jnp.int32), axis=0) - 1
        place = jnp.where(named, place, -1).T
        return place[:, None, :] == jnp.arange(cap)[None, :, None]

    lanes = (channels // 128, 128)
    signal = mixer_input.astype(f32).reshape(tokens, *lanes)
    step = step_size.reshape(tokens, *lanes)
    rate = (decay_rate * (-1.0 / math.log(2.0))).reshape(states, *lanes)
    into, outof = state_in.reshape(-1), state_out.reshape(-1)
    plain = pltpu.CompilerParams(vmem_limit_bytes=VMEM_LIMIT)
    ends = pl.pallas_call(
        functools.partial(ends_kernel, slab_len, prompts, states),
        out_shape=jax.ShapeDtypeStruct((prompts, states + 1) + lanes, f32),
        in_specs=[LOCAL, LOCAL, LOCAL, SMEM],
        out_specs=LOCAL,
        compiler_params=plain,
    )(step, signal, rate, into)
    ends = gather_ctx(ends, (n_ctx,) + ends.shape, n_ctx, block, 1)
    entering = jnp.zeros((prompts, states) + lanes, f32)
    for j in range(n_ctx - 1):
        longer = jnp.exp2(ends[j, :, states:] * rate[None]) * entering + ends[j, :, :states]
        entering = jnp.where(j < ctx, longer, entering)
    output = pl.pallas_call(
        functools.partial(scan_kernel, slab_len, prompts, states),
        out_shape=jax.ShapeDtypeStruct((tokens,) + lanes, f32),
        in_specs=[LOCAL, LOCAL, LOCAL, SMEM, SMEM, LOCAL],
        out_specs=LOCAL,
        compiler_params=plain,
    )(step, signal, rate, into, outof, entering)
    output = output.reshape(tokens, channels) + skip * mixer_input.astype(f32).reshape(tokens, -1)
    mixed = (output * jax.nn.silu(gate_in.astype(f32).reshape(tokens, -1))).astype(bf16)

    mixed = gather_ctx(
        mixed, (n_ctx * tokens, channels), n_ctx,
        lambda ref, c: ref.at[pl.ds(pl.multiple_of(c * tokens, tokens), tokens)], 2,
    )
    partial_value = jnp.dot(mixed, out_proj, preferred_element_type=f32).astype(bf16)
    partial_value = partial_value.reshape(n_ctx, tokens, halves, share).transpose(0, 2, 1, 3)
    projected = scatter_sum(partial_value.reshape(n_exp, tokens, share), "exp", n_exp, 3)
    residual = hidden.astype(f32) + projected
    residual_home = lax.ppermute(residual, ("ctx", "exp"), swap)

    chosen = selector(lax.dynamic_index_in_dim(routes, slab, 0, keepdims=False))
    rows = jnp.dot(
        chosen.astype(bf16).reshape(n_exp * cap, tokens),
        residual.astype(bf16),
        preferred_element_type=f32,
    ).astype(bf16)
    whole_axis = (lambda me, r: r, lambda me: me)

    def landing(ref, e):
        s, h = e // halves, lax.rem(e, halves)
        return ref.at[
            pl.ds(pl.multiple_of(s * cap, cap), cap), pl.ds(pl.multiple_of(h * share, share), share)
        ]

    rows = exchange(
        rows.reshape(n_exp, cap, share), (n_ctx * cap, halves * share), "exp", n_exp, *whole_axis,
        block, landing, 5,
    )
    span = halves * share
    rows = gather_ctx(
        rows, (n_ctx * cap, n_ctx * span), n_ctx,
        lambda ref, c: ref.at[:, pl.ds(pl.multiple_of(c * span, span), span)], 6,
    )
    rows = rows.astype(f32)
    scale = lax.rsqrt(jnp.mean(rows * rows, axis=1, keepdims=True) + epsilon)
    segment = (rows * scale * norm_gain).astype(bf16)

    gate_part = jnp.dot(segment, w_gate[0], preferred_element_type=f32)
    up_part = jnp.dot(segment, w_up[0], preferred_element_type=f32)
    activ = (jax.nn.silu(gate_part) * up_part).astype(bf16)
    down = jnp.dot(activ, w_down[0], preferred_element_type=f32).astype(bf16)
    returned = scatter_sum(down.reshape(n_ctx, cap, -1), "ctx", n_ctx, 7)

    own = selector(route_ids.reshape(tokens, -1))
    weights = route_weight.reshape(tokens, -1)
    strength = jnp.sum(jnp.where(route_ids.reshape(tokens, -1) == exp, weights, 0.0), axis=1)
    mine = lax.dynamic_index_in_dim(own, exp, 0, keepdims=False)
    slot_weight = jnp.sum(jnp.where(mine, strength[None, :], 0.0), axis=1)
    contrib = (returned * slot_weight[:, None]).astype(bf16)
    back = exchange(
        contrib, (n_exp, cap, share), "exp", n_exp, *whole_axis,
        lambda ref, e: ref.at[:, pl.ds(pl.multiple_of(e * share, share), share)], block, 9,
    )
    combined = lax.dot_general(
        own.astype(bf16).reshape(n_exp * cap, tokens),
        back.reshape(n_exp * cap, share),
        (((0,), (0,)), ((), ())),
        preferred_element_type=f32,
    )
    return (residual_home + combined).astype(bf16).reshape(slab_len, prompts, share)


def solution(mesh):
    placed = (
        P("ctx", None, "exp"),
        P("ctx", None, "exp"),
        P("ctx", None, "exp"),
        P(None, "exp"),
        P("ctx", None, None),
        P("ctx", None, None),
        P("exp"),
        P("exp", "ctx"),
        P("ctx", None, "exp"),
        P(),
        P("exp", None, "ctx"),
        P("exp", None, "ctx"),
        P("exp", "ctx", None),
        P("ctx", None, None),
        P("ctx", None, None),
    )
    return jax.shard_map(
        on_device, mesh=mesh, in_specs=placed, out_specs=P("ctx", None, "exp"), check_vma=False
    )
```

```python
import functools
import math

import jax
import jax.numpy as jnp
from jax import lax
from jax.experimental import pallas as pl
from jax.experimental.pallas import tpu as pltpu
from jax.sharding import PartitionSpec as P

epsilon = 1e-06
f32, bf16 = jnp.float32, jnp.bfloat16
MESH = pl.DeviceIdType.MESH
VMEM_LIMIT = 48 * 1024 * 1024
SMEM = pl.BlockSpec(memory_space=pltpu.SMEM)
LOCAL = pl.BlockSpec(memory_space=pltpu.VMEM)


def factors(count):
    inner = 2 ** (count.bit_length() // 2 - (1 if count.bit_length() % 2 == 0 else 0))
    return count // inner, inner


def ends_kernel(length, prompts, states, step_ref, signal_ref, rate_ref, into_ref, end_ref):
    tile = step_ref.shape[1:]
    for b in range(prompts):

        def chunk(i, carry):
            held, total = carry
            for u in range(4):
                row = (i * 4 + u) * prompts + b
                step = step_ref[row]
                inflow = step * signal_ref[row]
                held = tuple(
                    jnp.exp2(step * rate_ref[n]) * held[n] + inflow * into_ref[row * states + n]
                    for n in range(states)
                )
                total = total + step
            return held, total

        zero = jnp.zeros(tile, f32)
        held, total = lax.fori_loop(0, length // 4, chunk, ((zero,) * states, zero))
        for n in range(states):
            end_ref[b, n] = held[n]
        end_ref[b, states] = total


def scan_kernel(
    length, prompts, states, step_ref, signal_ref, rate_ref, into_ref, outof_ref, enter_ref, out_ref
):
    for b in range(prompts):

        def chunk(i, held):
            for u in range(4):
                row = (i * 4 + u) * prompts + b
                step = step_ref[row]
                inflow = step * signal_ref[row]
                held = tuple(
                    jnp.exp2(step * rate_ref[n]) * held[n] + inflow * into_ref[row * states + n]
                    for n in range(states)
                )
                terms = [held[n] * outof_ref[row * states + n] for n in range(states)]
                while len(terms) > 1:
                    terms = [p + q for p, q in zip(terms[::2], terms[1::2])]
                out_ref[row] = terms[0]
            return held

        lax.fori_loop(0, length // 4, chunk, tuple(enter_ref[b, n] for n in range(states)))


def wave(barrier, peers):
    for where in peers:
        pl.semaphore_signal(barrier, inc=1, device_id=where, device_id_type=MESH)
    pl.semaphore_wait(barrier, len(peers))


def push(src, dst, send_sem, recv_sem, where):
    copy = pltpu.make_async_remote_copy(
        src_ref=src,
        dst_ref=dst,
        send_sem=send_sem,
        recv_sem=recv_sem,
        device_id=where,
        device_id_type=MESH,
    )
    copy.start()
    return copy


def lanes_of(index, width):
    return pl.ds(pl.multiple_of(index * width, width), width)


def sending(kernel, out_shape, dtype, scratch, ident, *operands):
    return pl.pallas_call(
        kernel,
        out_shape=jax.ShapeDtypeStruct(out_shape, dtype),
        in_specs=[LOCAL] * len(operands),
        out_specs=LOCAL,
        scratch_shapes=scratch,
        compiler_params=pltpu.CompilerParams(
            collective_id=ident, has_side_effects=True, vmem_limit_bytes=VMEM_LIMIT
        ),
    )(*operands)


def gather_ctx(x, out_shape, count, target, ident):
    chips = count // 2

    def kernel(x_ref, o_ref, send_sem, recv_sem):
        me = lax.axis_index("ctx")
        chip, core = me // 2, lax.rem(me, 2)
        twin = {"ctx": chip * 2 + (1 - core)}
        others = [{"ctx": lax.rem(chip + k, chips) * 2 + core} for k in range(1, chips)]
        wave(pltpu.get_barrier_semaphore(), [twin] + others)
        across = [
            push(x_ref, target(o_ref, me), send_sem.at[k], recv_sem.at[k], others[k - 1])
            for k in range(1, chips)
        ]
        pending = [push(x_ref, target(o_ref, me), send_sem.at[0], recv_sem.at[0], twin)]
        target(o_ref, me)[...] = x_ref[...]
        for k in range(1, chips):
            across[k - 1].wait_recv()
            view = target(o_ref, lax.rem(chip + chips - k, chips) * 2 + core)
            slot = chips - 1 + k
            pending.append(push(view, view, send_sem.at[slot], recv_sem.at[slot], twin))
        for copy in across:
            copy.wait_send()
        for copy in pending:
            copy.wait()

    slots = pltpu.SemaphoreType.DMA((2 * chips - 1,))
    return sending(kernel, out_shape, x.dtype, [slots, slots], ident, x)


def scatter_sum(x, tokens, width, halves, count, parts, ident):
    outer, inner = factors(count)
    rows = tokens // parts

    def kernel(x_ref, o_ref, got1, part, got2, send1, recv1, send2, recv2):
        me = lax.axis_index("exp")
        o_me, i_me = me // inner, lax.rem(me, inner)
        near = [{"exp": o_me * inner + lax.rem(i_me + k, inner)} for k in range(1, inner)]
        far = [{"exp": lax.rem(o_me + j, outer) * inner + i_me} for j in range(1, outer)]
        wave(pltpu.get_barrier_semaphore(), near + far)

        def view(o, i, p):
            e = o * inner + i
            first = pl.multiple_of((e // halves) * tokens + p * rows, rows)
            return x_ref.at[pl.ds(first, rows), lanes_of(lax.rem(e, halves), width)]

        order = [(j % outer, p) for j in range(1, outer + 1) for p in range(parts)]
        first, sent = {}, []
        for j, p in order:
            for k in range(1, inner):
                copy = push(
                    view(lax.rem(o_me + j, outer), lax.rem(i_me + k, inner), p),
                    got1.at[k - 1, j, p],
                    send1.at[k - 1, j, p],
                    recv1.at[k - 1, j, p],
                    near[k - 1],
                )
                first[k, j, p] = copy
                sent.append(copy)

        def near_sum(j, p):
            total = view(lax.rem(o_me + j, outer), i_me, p)[...].astype(f32)
            for k in range(1, inner):
                first[k, j, p].wait_recv()
                total = total + got1[k - 1, j, p].astype(f32)
            return total

        second = {}
        for j, p in order:
            if j == 0:
                continue
            part[j - 1, p] = near_sum(j, p).astype(bf16)
            second[j, p] = push(
                part.at[j - 1, p],
                got2.at[j - 1, p],
                send2.at[j - 1, p],
                recv2.at[j - 1, p],
                far[j - 1],
            )
            sent.append(second[j, p])
        for p in range(parts):
            total = near_sum(0, p)
            for j in range(1, outer):
                second[j, p].wait_recv()
                total = total + got2[j - 1, p].astype(f32)
            o_ref[p * rows : (p + 1) * rows] = total
        for copy in sent:
            copy.wait_send()

    sem1 = pltpu.SemaphoreType.DMA((inner - 1, outer, parts))
    sem2 = pltpu.SemaphoreType.DMA((outer - 1, parts))
    scratch = [
        pltpu.VMEM((inner - 1, outer, parts, rows, width), bf16),
        pltpu.VMEM((outer - 1, parts, rows, width), bf16),
        pltpu.VMEM((outer - 1, parts, rows, width), bf16),
        sem1, sem1, sem2, sem2,
    ]
    return sending(kernel, (tokens, width), f32, scratch, ident, x)


def dispatch(x, n_ctx, n_exp, ident):
    _, cap, width = x.shape
    halves, chips = n_exp // n_ctx, n_ctx // 2

    def kernel(x_ref, o_ref, s_in, r_in, s_twin, r_twin, s_far, r_far, s_fwd, r_fwd):
        ctx, me = lax.axis_index("ctx"), lax.axis_index("exp")
        chip, core = ctx // 2, lax.rem(ctx, 2)
        twin = {"ctx": chip * 2 + (1 - core)}
        others = [{"ctx": lax.rem(chip + k, chips) * 2 + core} for k in range(1, chips)]
        peers = [{"exp": lax.rem(me + k, n_exp)} for k in range(1, n_exp)]
        wave(pltpu.get_barrier_semaphore(), [twin] + others + peers)

        def view(c, e):
            first = pl.multiple_of((e // halves) * cap, cap)
            return o_ref.at[pl.ds(first, cap), lanes_of(c * halves + lax.rem(e, halves), width)]

        arriving = [
            push(
                x_ref.at[lax.rem(me + k, n_exp)], view(ctx, me),
                s_in.at[k - 1], r_in.at[k - 1], peers[k - 1],
            )
            for k in range(1, n_exp)
        ]
        view(ctx, me)[...] = x_ref[me]
        far, near = {}, []
        for j in range(n_exp):
            if j:
                arriving[j - 1].wait_recv()
            mine = view(ctx, lax.rem(me + n_exp - j, n_exp))
            for k in range(1, chips):
                far[k, j] = push(
                    mine, mine, s_far.at[k - 1, j], r_far.at[k - 1, j], others[k - 1]
                )
            near.append(push(mine, mine, s_twin.at[j], r_twin.at[j], twin))
        for j in range(n_exp):
            for k in range(1, chips):
                far[k, j].wait_recv()
                owner = lax.rem(chip + chips - k, chips) * 2 + core
                theirs = view(owner, lax.rem(me + n_exp - j, n_exp))
                near.append(push(theirs, theirs, s_fwd.at[k - 1, j], r_fwd.at[k - 1, j], twin))
        for copy in arriving + list(far.values()):
            copy.wait_send()
        for copy in near:
            copy.wait()

    sem_in = pltpu.SemaphoreType.DMA((n_exp - 1,))
    sem_twin = pltpu.SemaphoreType.DMA((n_exp,))
    sem_far = pltpu.SemaphoreType.DMA((chips - 1, n_exp))
    scratch = [sem_in, sem_in, sem_twin, sem_twin, sem_far, sem_far, sem_far, sem_far]
    return sending(kernel, (n_ctx * cap, n_exp * width), x.dtype, scratch, ident, x)


def combine(x, weight, n_ctx, n_exp, ident):
    _, cap, features = x.shape
    width, chips = features // n_exp, n_ctx // 2

    def kernel(x_ref, w_ref, o_ref, got1, part, got2, ready, s1, r1, s2, r2, s3, r3):
        ctx, me = lax.axis_index("ctx"), lax.axis_index("exp")
        chip, core = ctx // 2, lax.rem(ctx, 2)
        twin = {"ctx": chip * 2 + (1 - core)}
        others = [{"ctx": lax.rem(chip + k, chips) * 2 + core} for k in range(1, chips)]
        peers = [{"exp": lax.rem(me + k, n_exp)} for k in range(1, n_exp)]
        wave(pltpu.get_barrier_semaphore(), [twin] + others + peers)
        columns = [lanes_of(lax.rem(me + j, n_exp), width) for j in range(n_exp)]
        turns = list(range(1, n_exp)) + [0]
        first, sent = {}, []
        for j in turns:
            for k in [*range(1, chips), 0]:
                block = lax.rem(chip + k, chips) * 2 + (1 - core)
                first[j, k] = push(
                    x_ref.at[block, :, columns[j]], got1.at[k, :, columns[j]],
                    s1.at[j, k], r1.at[j, k], twin,
                )
                sent.append(first[j, k])

        def near_sum(j, k):
            first[j, k].wait_recv()
            block = lax.rem(chip + k, chips) * 2 + core
            return x_ref[block, :, columns[j]].astype(f32) + got1[k, :, columns[j]].astype(f32)

        second = {}
        for j in turns:
            for k in range(1, chips):
                part[k - 1, :, columns[j]] = near_sum(j, k).astype(bf16)
                second[j, k] = push(
                    part.at[k - 1, :, columns[j]], got2.at[k - 1, :, columns[j]],
                    s2.at[j, k - 1], r2.at[j, k - 1], others[k - 1],
                )
                sent.append(second[j, k])
        last = []
        for j in turns:
            total = near_sum(j, 0)
            for k in range(1, chips):
                second[j, k].wait_recv()
                total = total + got2[k - 1, :, columns[j]].astype(f32)
            total = (total * w_ref[...]).astype(bf16)
            if j:
                ready[j - 1] = total
                last.append(
                    push(ready.at[j - 1], o_ref.at[me], s3.at[j - 1], r3.at[j - 1], peers[j - 1])
                )
            else:
                o_ref[me] = total
        for copy in sent:
            copy.wait_send()
        for copy in last:
            copy.wait()

    sem1 = pltpu.SemaphoreType.DMA((n_exp, chips))
    sem2 = pltpu.SemaphoreType.DMA((n_exp, chips - 1))
    sem3 = pltpu.SemaphoreType.DMA((n_exp - 1,))
    scratch = [
        pltpu.VMEM((chips, cap, features), bf16),
        pltpu.VMEM((chips - 1, cap, features), bf16),
        pltpu.VMEM((chips - 1, cap, features), bf16),
        pltpu.VMEM((n_exp - 1, cap, width), bf16),
        sem1, sem1, sem2, sem2, sem3, sem3,
    ]
    return sending(kernel, (n_exp, cap, width), bf16, scratch, ident, x, weight)


def block(ref, r):
    return ref.at[r]


def on_device(
    mixer_input,
    gate_in,
    step_size,
    decay_rate,
    state_in,
    state_out,
    skip,
    out_proj,
    hidden_in,
    norm_gain,
    w_gate,
    w_up,
    w_down,
    route_ids,
    route_weight,
):
    slab_len, prompts, channels = mixer_input.shape
    states = decay_rate.shape[0]
    tokens = slab_len * prompts
    n_ctx, n_exp = lax.axis_size("ctx"), lax.axis_size("exp")
    ctx, exp = lax.axis_index("ctx"), lax.axis_index("exp")
    share = hidden_in.shape[-1]
    halves = n_exp // n_ctx
    cap = 4 * tokens // (w_gate.shape[0] * n_exp)

    swap = [
        (c * n_exp + e, (e // halves) * n_exp + c * halves + e % halves)
        for c in range(n_ctx)
        for e in range(n_exp)
    ]
    hidden = lax.ppermute(hidden_in.reshape(tokens, share), ("ctx", "exp"), swap)
    routes = lax.all_gather(route_ids.reshape(tokens, -1), "ctx", axis=0)
    slab = exp // halves

    def selector(routed):
        named = jnp.any(routed[:, :, None] == jnp.arange(n_exp)[None, None, :], axis=1)
        place = jnp.cumsum(named.astype(jnp.int32), axis=0) - 1
        place = jnp.where(named, place, -1).T
        return place[:, None, :] == jnp.arange(cap)[None, :, None]

    lanes = (channels // 128, 128)
    signal = mixer_input.astype(f32).reshape(tokens, *lanes)
    step = step_size.reshape(tokens, *lanes)
    rate = (decay_rate * (-1.0 / math.log(2.0))).reshape(states, *lanes)
    into, outof = state_in.reshape(-1), state_out.reshape(-1)
    plain = pltpu.CompilerParams(vmem_limit_bytes=VMEM_LIMIT)
    ends = pl.pallas_call(
        functools.partial(ends_kernel, slab_len, prompts, states),
        out_shape=jax.ShapeDtypeStruct((prompts, states + 1) + lanes, f32),
        in_specs=[LOCAL, LOCAL, LOCAL, SMEM],
        out_specs=LOCAL,
        compiler_params=plain,
    )(step, signal, rate, into)
    ends = gather_ctx(ends, (n_ctx,) + ends.shape, n_ctx, block, 1)
    entering = jnp.zeros((prompts, states) + lanes, f32)
    for j in range(n_ctx - 1):
        longer = jnp.exp2(ends[j, :, states:] * rate[None]) * entering + ends[j, :, :states]
        entering = jnp.where(j < ctx, longer, entering)
    output = pl.pallas_call(
        functools.partial(scan_kernel, slab_len, prompts, states),
        out_shape=jax.ShapeDtypeStruct((tokens,) + lanes, f32),
        in_specs=[LOCAL, LOCAL, LOCAL, SMEM, SMEM, LOCAL],
        out_specs=LOCAL,
        compiler_params=plain,
    )(step, signal, rate, into, outof, entering)
    output = output.reshape(tokens, channels) + skip * mixer_input.astype(f32).reshape(tokens, -1)
    mixed = (output * jax.nn.silu(gate_in.astype(f32).reshape(tokens, -1))).astype(bf16)

    mixed = gather_ctx(
        mixed, (n_ctx * tokens, channels), n_ctx,
        lambda ref, c: ref.at[pl.ds(pl.multiple_of(c * tokens, tokens), tokens)], 2,
    )
    partial_value = jnp.dot(mixed, out_proj, preferred_element_type=f32).astype(bf16)
    projected = scatter_sum(partial_value, tokens, share, halves, n_exp, 2, 3)
    residual = hidden.astype(f32) + projected

    chosen = selector(lax.dynamic_index_in_dim(routes, slab, 0, keepdims=False))
    rows = jnp.dot(
        chosen.astype(bf16).reshape(n_exp * cap, tokens),
        residual.astype(bf16),
        preferred_element_type=f32,
    ).astype(bf16)
    rows = dispatch(rows.reshape(n_exp, cap, share), n_ctx, n_exp, 4)
    rows, residual = lax.optimization_barrier((rows, residual))
    residual_home = lax.ppermute(residual, ("ctx", "exp"), swap)
    rows = rows.astype(f32)
    scale = lax.rsqrt(jnp.mean(rows * rows, axis=1, keepdims=True) + epsilon)
    segment = (rows * scale * norm_gain).astype(bf16)

    gate_part = jnp.dot(segment, w_gate[0], preferred_element_type=f32)
    up_part = jnp.dot(segment, w_up[0], preferred_element_type=f32)
    activ = (jax.nn.silu(gate_part) * up_part).astype(bf16)
    down = jnp.dot(activ, w_down[0], preferred_element_type=f32).astype(bf16)

    own = selector(route_ids.reshape(tokens, -1))
    weights = route_weight.reshape(tokens, -1)
    strength = jnp.sum(jnp.where(route_ids.reshape(tokens, -1) == exp, weights, 0.0), axis=1)
    mine = lax.dynamic_index_in_dim(own, exp, 0, keepdims=False)
    slot_weight = jnp.sum(jnp.where(mine, strength[None, :], 0.0), axis=1)
    slot_weight = jnp.broadcast_to(slot_weight[:, None], (cap, share))
    back = combine(down.reshape(n_ctx, cap, -1), slot_weight, n_ctx, n_exp, 5)
    combined = lax.dot_general(
        own.astype(bf16).reshape(n_exp * cap, tokens),
        back.reshape(n_exp * cap, share),
        (((0,), (0,)), ((), ())),
        preferred_element_type=f32,
    )
    return (residual_home + combined).astype(bf16).reshape(slab_len, prompts, share)


def solution(mesh):
    placed = (
        P("ctx", None, "exp"),
        P("ctx", None, "exp"),
        P("ctx", None, "exp"),
        P(None, "exp"),
        P("ctx", None, None),
        P("ctx", None, None),
        P("exp"),
        P("exp", "ctx"),
        P("ctx", None, "exp"),
        P(),
        P("exp", None, "ctx"),
        P("exp", None, "ctx"),
        P("exp", "ctx", None),
        P("ctx", None, None),
        P("ctx", None, None),
    )
    return jax.shard_map(
        on_device, mesh=mesh, in_specs=placed, out_specs=P("ctx", None, "exp"), check_vma=False
    )
```

```python
import functools
import math

import jax
import jax.numpy as jnp
from jax import lax
from jax.experimental import pallas as pl
from jax.experimental.pallas import tpu as pltpu
from jax.sharding import PartitionSpec as P

epsilon = 1e-06
f32, bf16 = jnp.float32, jnp.bfloat16
MESH = pl.DeviceIdType.MESH
VMEM_LIMIT = 48 * 1024 * 1024
SMEM = pl.BlockSpec(memory_space=pltpu.SMEM)
LOCAL = pl.BlockSpec(memory_space=pltpu.VMEM)


def factors(count):
    inner = 2 ** (count.bit_length() // 2 - (1 if count.bit_length() % 2 == 0 else 0))
    return count // inner, inner


def ends_kernel(
    length, prompts, states, step_ref, signal_ref, rate_ref, into_ref, route_ref, end_ref
):
    tile = step_ref.shape[1:]
    for b in range(prompts):

        def chunk(i, carry):
            held, total = carry
            for u in range(4):
                row = (i * 4 + u) * prompts + b
                step = step_ref[row]
                inflow = step * signal_ref[row]
                held = tuple(
                    jnp.exp2(step * rate_ref[n]) * held[n] + inflow * into_ref[row * states + n]
                    for n in range(states)
                )
                total = total + step
            return held, total

        zero = jnp.zeros(tile, f32)
        held, total = lax.fori_loop(0, length // 4, chunk, ((zero,) * states, zero))
        for n in range(states):
            end_ref[b * (states + 1) + n] = held[n]
        end_ref[b * (states + 1) + states] = total
    end_ref[prompts * (states + 1) :] = route_ref[...]


def scan_kernel(
    length, prompts, states, step_ref, signal_ref, rate_ref, into_ref, outof_ref, enter_ref, out_ref
):
    for b in range(prompts):

        def chunk(i, held):
            for u in range(4):
                row = (i * 4 + u) * prompts + b
                step = step_ref[row]
                inflow = step * signal_ref[row]
                held = tuple(
                    jnp.exp2(step * rate_ref[n]) * held[n] + inflow * into_ref[row * states + n]
                    for n in range(states)
                )
                terms = [held[n] * outof_ref[row * states + n] for n in range(states)]
                while len(terms) > 1:
                    terms = [p + q for p, q in zip(terms[::2], terms[1::2])]
                out_ref[row] = terms[0]
            return held

        lax.fori_loop(0, length // 4, chunk, tuple(enter_ref[b, n] for n in range(states)))


def act_kernel(rows_ref, gain_ref, gate_ref, up_ref, out_ref, normed):
    count, features = rows_ref.shape

    @pl.when(pl.program_id(0) == 0)
    def _():
        def norm(i, _):
            here = pl.ds(pl.multiple_of(i * 32, 32), 32)
            rows = rows_ref[here].astype(f32)
            scale = lax.rsqrt(jnp.sum(rows * rows, axis=1, keepdims=True) / features + epsilon)
            normed[here] = (rows * scale * gain_ref[...]).astype(bf16)
            return 0

        lax.fori_loop(0, count // 32, norm, 0)

    gate_part = jnp.dot(normed[...], gate_ref[0], preferred_element_type=f32)
    up_part = jnp.dot(normed[...], up_ref[0], preferred_element_type=f32)
    out_ref[...] = (gate_part / (1.0 + jnp.exp(-gate_part)) * up_part).astype(bf16)


def expert_act(rows, gain, w_gate, w_up):
    count, features = rows.shape
    hidden = w_gate.shape[2]
    tile = 256 if hidden % 256 == 0 else 128
    weights = pl.BlockSpec((1, features, tile), lambda i: (0, 0, i))
    return pl.pallas_call(
        act_kernel,
        grid=(hidden // tile,),
        out_shape=jax.ShapeDtypeStruct((count, hidden), bf16),
        in_specs=[
            pl.BlockSpec((count, features), lambda i: (0, 0)),
            pl.BlockSpec((1, features), lambda i: (0, 0)),
            weights,
            weights,
        ],
        out_specs=pl.BlockSpec((count, tile), lambda i: (0, i)),
        scratch_shapes=[pltpu.VMEM((count, features), bf16)],
        compiler_params=pltpu.CompilerParams(vmem_limit_bytes=VMEM_LIMIT),
    )(rows, gain, w_gate, w_up)


def down_kernel(act_ref, weight_ref, out_ref):
    out_ref[...] = jnp.dot(
        act_ref[...], weight_ref[0], preferred_element_type=f32
    ).astype(bf16)


def expert_down(activ, w_down):
    count, hidden = activ.shape
    features = w_down.shape[2]
    return pl.pallas_call(
        down_kernel,
        grid=(features // 512,),
        out_shape=jax.ShapeDtypeStruct((count, features), bf16),
        in_specs=[
            pl.BlockSpec((count, hidden), lambda i: (0, 0)),
            pl.BlockSpec((1, hidden, 512), lambda i: (0, 0, i)),
        ],
        out_specs=pl.BlockSpec((count, 512), lambda i: (0, i)),
        compiler_params=pltpu.CompilerParams(vmem_limit_bytes=VMEM_LIMIT),
    )(activ, w_down)


def wave(barrier, peers):
    for where in peers:
        pl.semaphore_signal(barrier, inc=1, device_id=where, device_id_type=MESH)
    pl.semaphore_wait(barrier, len(peers))


def push(src, dst, send_sem, recv_sem, where):
    copy = pltpu.make_async_remote_copy(
        src_ref=src,
        dst_ref=dst,
        send_sem=send_sem,
        recv_sem=recv_sem,
        device_id=where,
        device_id_type=MESH,
    )
    copy.start()
    return copy


def lanes_of(index, width):
    return pl.ds(pl.multiple_of(index * width, width), width)


def sending(kernel, out_shape, dtype, scratch, ident, *operands):
    return pl.pallas_call(
        kernel,
        out_shape=jax.ShapeDtypeStruct(out_shape, dtype),
        in_specs=[LOCAL] * len(operands),
        out_specs=LOCAL,
        scratch_shapes=scratch,
        compiler_params=pltpu.CompilerParams(
            collective_id=ident, has_side_effects=True, vmem_limit_bytes=VMEM_LIMIT
        ),
    )(*operands)


def gather_ctx(x, out_shape, count, target, ident):
    chips = count // 2

    def kernel(x_ref, o_ref, send_sem, recv_sem):
        me = lax.axis_index("ctx")
        chip, core = me // 2, lax.rem(me, 2)
        twin = {"ctx": chip * 2 + (1 - core)}
        others = [{"ctx": lax.rem(chip + k, chips) * 2 + core} for k in range(1, chips)]
        wave(pltpu.get_barrier_semaphore(), [twin] + others)
        across = [
            push(x_ref, target(o_ref, me), send_sem.at[k], recv_sem.at[k], others[k - 1])
            for k in range(1, chips)
        ]
        pending = [push(x_ref, target(o_ref, me), send_sem.at[0], recv_sem.at[0], twin)]
        target(o_ref, me)[...] = x_ref[...]
        for k in range(1, chips):
            across[k - 1].wait_recv()
            view = target(o_ref, lax.rem(chip + chips - k, chips) * 2 + core)
            slot = chips - 1 + k
            pending.append(push(view, view, send_sem.at[slot], recv_sem.at[slot], twin))
        for copy in across:
            copy.wait_send()
        for copy in pending:
            copy.wait()

    slots = pltpu.SemaphoreType.DMA((2 * chips - 1,))
    return sending(kernel, out_shape, x.dtype, [slots, slots], ident, x)


def scatter_sum(x, tokens, width, halves, count, parts, ident):
    outer, inner = factors(count)
    rows = tokens // parts

    def kernel(x_ref, o_ref, got1, part, got2, send1, recv1, send2, recv2):
        me = lax.axis_index("exp")
        o_me, i_me = me // inner, lax.rem(me, inner)
        near = [{"exp": o_me * inner + lax.rem(i_me + k, inner)} for k in range(1, inner)]
        far = [{"exp": lax.rem(o_me + j, outer) * inner + i_me} for j in range(1, outer)]
        wave(pltpu.get_barrier_semaphore(), near + far)

        def view(o, i, p):
            e = o * inner + i
            first = pl.multiple_of((e // halves) * tokens + p * rows, rows)
            return x_ref.at[pl.ds(first, rows), lanes_of(lax.rem(e, halves), width)]

        order = [(j % outer, p) for j in range(1, outer + 1) for p in range(parts)]
        first, sent = {}, []
        for j, p in order:
            for k in range(1, inner):
                copy = push(
                    view(lax.rem(o_me + j, outer), lax.rem(i_me + k, inner), p),
                    got1.at[k - 1, j, p],
                    send1.at[k - 1, j, p],
                    recv1.at[k - 1, j, p],
                    near[k - 1],
                )
                first[k, j, p] = copy
                sent.append(copy)

        def near_sum(j, p):
            total = view(lax.rem(o_me + j, outer), i_me, p)[...].astype(f32)
            for k in range(1, inner):
                first[k, j, p].wait_recv()
                total = total + got1[k - 1, j, p].astype(f32)
            return total

        second = {}
        for j, p in order:
            if j == 0:
                continue
            part[j - 1, p] = near_sum(j, p).astype(bf16)
            second[j, p] = push(
                part.at[j - 1, p],
                got2.at[j - 1, p],
                send2.at[j - 1, p],
                recv2.at[j - 1, p],
                far[j - 1],
            )
            sent.append(second[j, p])
        for p in range(parts):
            total = near_sum(0, p)
            for j in range(1, outer):
                second[j, p].wait_recv()
                total = total + got2[j - 1, p].astype(f32)
            o_ref[p * rows : (p + 1) * rows] = total
        for copy in sent:
            copy.wait_send()

    sem1 = pltpu.SemaphoreType.DMA((inner - 1, outer, parts))
    sem2 = pltpu.SemaphoreType.DMA((outer - 1, parts))
    scratch = [
        pltpu.VMEM((inner - 1, outer, parts, rows, width), bf16),
        pltpu.VMEM((outer - 1, parts, rows, width), bf16),
        pltpu.VMEM((outer - 1, parts, rows, width), bf16),
        sem1, sem1, sem2, sem2,
    ]
    return sending(kernel, (tokens, width), f32, scratch, ident, x)


def dispatch(x, n_ctx, n_exp, ident):
    _, cap, width = x.shape
    halves, chips = n_exp // n_ctx, n_ctx // 2

    def kernel(x_ref, o_ref, s_in, r_in, s_twin, r_twin, s_far, r_far, s_fwd, r_fwd):
        ctx, me = lax.axis_index("ctx"), lax.axis_index("exp")
        chip, core = ctx // 2, lax.rem(ctx, 2)
        twin = {"ctx": chip * 2 + (1 - core)}
        others = [{"ctx": lax.rem(chip + k, chips) * 2 + core} for k in range(1, chips)]
        peers = [{"exp": lax.rem(me + k, n_exp)} for k in range(1, n_exp)]
        wave(pltpu.get_barrier_semaphore(), [twin] + others + peers)

        def view(c, e):
            first = pl.multiple_of((e // halves) * cap, cap)
            return o_ref.at[pl.ds(first, cap), lanes_of(c * halves + lax.rem(e, halves), width)]

        arriving = [
            push(
                x_ref.at[lax.rem(me + k, n_exp)], view(ctx, me),
                s_in.at[k - 1], r_in.at[k - 1], peers[k - 1],
            )
            for k in range(1, n_exp)
        ]
        view(ctx, me)[...] = x_ref[me]
        far, near = {}, []
        for j in range(n_exp):
            if j:
                arriving[j - 1].wait_recv()
            mine = view(ctx, lax.rem(me + n_exp - j, n_exp))
            for k in range(1, chips):
                far[k, j] = push(
                    mine, mine, s_far.at[k - 1, j], r_far.at[k - 1, j], others[k - 1]
                )
            near.append(push(mine, mine, s_twin.at[j], r_twin.at[j], twin))
        for j in range(n_exp):
            for k in range(1, chips):
                far[k, j].wait_recv()
                owner = lax.rem(chip + chips - k, chips) * 2 + core
                theirs = view(owner, lax.rem(me + n_exp - j, n_exp))
                near.append(push(theirs, theirs, s_fwd.at[k - 1, j], r_fwd.at[k - 1, j], twin))
        for copy in arriving + list(far.values()):
            copy.wait_send()
        for copy in near:
            copy.wait()

    sem_in = pltpu.SemaphoreType.DMA((n_exp - 1,))
    sem_twin = pltpu.SemaphoreType.DMA((n_exp,))
    sem_far = pltpu.SemaphoreType.DMA((chips - 1, n_exp))
    scratch = [sem_in, sem_in, sem_twin, sem_twin, sem_far, sem_far, sem_far, sem_far]
    return sending(kernel, (n_ctx * cap, n_exp * width), x.dtype, scratch, ident, x)


def combine(x, weight, n_ctx, n_exp, ident):
    _, cap, features = x.shape
    width, chips = features // n_exp, n_ctx // 2

    def kernel(x_ref, w_ref, o_ref, got1, part, got2, ready, s1, r1, s2, r2, s3, r3):
        ctx, me = lax.axis_index("ctx"), lax.axis_index("exp")
        chip, core = ctx // 2, lax.rem(ctx, 2)
        twin = {"ctx": chip * 2 + (1 - core)}
        others = [{"ctx": lax.rem(chip + k, chips) * 2 + core} for k in range(1, chips)]
        peers = [{"exp": lax.rem(me + k, n_exp)} for k in range(1, n_exp)]
        wave(pltpu.get_barrier_semaphore(), [twin] + others + peers)
        columns = [lanes_of(lax.rem(me + j, n_exp), width) for j in range(n_exp)]
        turns = list(range(1, n_exp)) + [0]
        first, sent = {}, []
        for j in turns:
            for k in [*range(1, chips), 0]:
                block = lax.rem(chip + k, chips) * 2 + (1 - core)
                first[j, k] = push(
                    x_ref.at[block, :, columns[j]], got1.at[k, :, columns[j]],
                    s1.at[j, k], r1.at[j, k], twin,
                )
                sent.append(first[j, k])

        def near_sum(j, k):
            first[j, k].wait_recv()
            block = lax.rem(chip + k, chips) * 2 + core
            return x_ref[block, :, columns[j]].astype(f32) + got1[k, :, columns[j]].astype(f32)

        second = {}
        for j in turns:
            for k in range(1, chips):
                part[k - 1, :, columns[j]] = near_sum(j, k).astype(bf16)
                second[j, k] = push(
                    part.at[k - 1, :, columns[j]], got2.at[k - 1, :, columns[j]],
                    s2.at[j, k - 1], r2.at[j, k - 1], others[k - 1],
                )
                sent.append(second[j, k])
        last = []
        for j in turns:
            total = near_sum(j, 0)
            for k in range(1, chips):
                second[j, k].wait_recv()
                total = total + got2[k - 1, :, columns[j]].astype(f32)
            total = (total * w_ref[...]).astype(bf16)
            if j:
                ready[j - 1] = total
                last.append(
                    push(ready.at[j - 1], o_ref.at[me], s3.at[j - 1], r3.at[j - 1], peers[j - 1])
                )
            else:
                o_ref[me] = total
        for copy in sent:
            copy.wait_send()
        for copy in last:
            copy.wait()

    sem1 = pltpu.SemaphoreType.DMA((n_exp, chips))
    sem2 = pltpu.SemaphoreType.DMA((n_exp, chips - 1))
    sem3 = pltpu.SemaphoreType.DMA((n_exp - 1,))
    scratch = [
        pltpu.VMEM((chips, cap, features), bf16),
        pltpu.VMEM((chips - 1, cap, features), bf16),
        pltpu.VMEM((chips - 1, cap, features), bf16),
        pltpu.VMEM((n_exp - 1, cap, width), bf16),
        sem1, sem1, sem2, sem2, sem3, sem3,
    ]
    return sending(kernel, (n_exp, cap, width), bf16, scratch, ident, x, weight)


def block(ref, r):
    return ref.at[r]


def on_device(
    mixer_input,
    gate_in,
    step_size,
    decay_rate,
    state_in,
    state_out,
    skip,
    out_proj,
    hidden_in,
    norm_gain,
    w_gate,
    w_up,
    w_down,
    route_ids,
    route_weight,
):
    slab_len, prompts, channels = mixer_input.shape
    states = decay_rate.shape[0]
    tokens = slab_len * prompts
    n_ctx, n_exp = lax.axis_size("ctx"), lax.axis_size("exp")
    ctx, exp = lax.axis_index("ctx"), lax.axis_index("exp")
    share = hidden_in.shape[-1]
    halves = n_exp // n_ctx
    cap = 4 * tokens // (w_gate.shape[0] * n_exp)

    swap = [
        (c * n_exp + e, (e // halves) * n_exp + c * halves + e % halves)
        for c in range(n_ctx)
        for e in range(n_exp)
    ]
    hidden = lax.ppermute(hidden_in.reshape(tokens, share), ("ctx", "exp"), swap)
    slab = exp // halves

    def selector(routed):
        named = jnp.any(routed[:, :, None] == jnp.arange(n_exp)[None, None, :], axis=1)
        place = jnp.cumsum(named.astype(jnp.int32), axis=0) - 1
        place = jnp.where(named, place, -1).T
        return place[:, None, :] == jnp.arange(cap)[None, :, None]

    lanes = (channels // 128, 128)
    signal = mixer_input.astype(f32).reshape(tokens, *lanes)
    step = step_size.reshape(tokens, *lanes)
    rate = (decay_rate * (-1.0 / math.log(2.0))).reshape(states, *lanes)
    into, outof = state_in.reshape(-1), state_out.reshape(-1)
    plain = pltpu.CompilerParams(vmem_limit_bytes=VMEM_LIMIT)
    named = route_ids.reshape(-1).astype(f32)
    named = jnp.pad(named, (0, -named.size % channels)).reshape(-1, *lanes)
    summary = prompts * (states + 1)
    ends = pl.pallas_call(
        functools.partial(ends_kernel, slab_len, prompts, states),
        out_shape=jax.ShapeDtypeStruct((summary + named.shape[0],) + lanes, f32),
        in_specs=[LOCAL, LOCAL, LOCAL, SMEM, LOCAL],
        out_specs=LOCAL,
        compiler_params=plain,
    )(step, signal, rate, into, named)
    ends = gather_ctx(ends, (n_ctx,) + ends.shape, n_ctx, block, 1)
    routes = ends[:, summary:].reshape(n_ctx, -1)[:, : route_ids.size].astype(jnp.int32)
    routes = routes.reshape(n_ctx, tokens, -1)
    ends = ends[:, :summary].reshape((n_ctx, prompts, states + 1) + lanes)
    entering = jnp.zeros((prompts, states) + lanes, f32)
    for j in range(n_ctx - 1):
        longer = jnp.exp2(ends[j, :, states:] * rate[None]) * entering + ends[j, :, :states]
        entering = jnp.where(j < ctx, longer, entering)
    output = pl.pallas_call(
        functools.partial(scan_kernel, slab_len, prompts, states),
        out_shape=jax.ShapeDtypeStruct((tokens,) + lanes, f32),
        in_specs=[LOCAL, LOCAL, LOCAL, SMEM, SMEM, LOCAL],
        out_specs=LOCAL,
        compiler_params=plain,
    )(step, signal, rate, into, outof, entering)
    output = output.reshape(tokens, channels) + skip * mixer_input.astype(f32).reshape(tokens, -1)
    mixed = (output * jax.nn.silu(gate_in.astype(f32).reshape(tokens, -1))).astype(bf16)

    mixed = gather_ctx(
        mixed, (n_ctx * tokens, channels), n_ctx,
        lambda ref, c: ref.at[pl.ds(pl.multiple_of(c * tokens, tokens), tokens)], 2,
    )
    partial_value = jnp.dot(mixed, out_proj, preferred_element_type=f32).astype(bf16)
    projected = scatter_sum(partial_value, tokens, share, halves, n_exp, 2, 3)
    residual = hidden.astype(f32) + projected

    chosen = selector(lax.dynamic_index_in_dim(routes, slab, 0, keepdims=False))
    rows = jnp.dot(
        chosen.astype(bf16).reshape(n_exp * cap, tokens),
        residual.astype(bf16),
        preferred_element_type=f32,
    ).astype(bf16)
    rows = dispatch(rows.reshape(n_exp, cap, share), n_ctx, n_exp, 4)
    rows, residual = lax.optimization_barrier((rows, residual))
    residual_home = lax.ppermute(residual, ("ctx", "exp"), swap)
    activ = expert_act(rows, norm_gain[None, :], w_gate, w_up)
    down = expert_down(activ, w_down)

    own = selector(route_ids.reshape(tokens, -1))
    weights = route_weight.reshape(tokens, -1)
    strength = jnp.sum(jnp.where(route_ids.reshape(tokens, -1) == exp, weights, 0.0), axis=1)
    mine = lax.dynamic_index_in_dim(own, exp, 0, keepdims=False)
    slot_weight = jnp.sum(jnp.where(mine, strength[None, :], 0.0), axis=1)
    slot_weight = jnp.broadcast_to(slot_weight[:, None], (cap, share))
    back = combine(down.reshape(n_ctx, cap, -1), slot_weight, n_ctx, n_exp, 5)
    combined = lax.dot_general(
        own.astype(bf16).reshape(n_exp * cap, tokens),
        back.reshape(n_exp * cap, share),
        (((0,), (0,)), ((), ())),
        preferred_element_type=f32,
    )
    return (residual_home + combined).astype(bf16).reshape(slab_len, prompts, share)


def solution(mesh):
    placed = (
        P("ctx", None, "exp"),
        P("ctx", None, "exp"),
        P("ctx", None, "exp"),
        P(None, "exp"),
        P("ctx", None, None),
        P("ctx", None, None),
        P("exp"),
        P("exp", "ctx"),
        P("ctx", None, "exp"),
        P(),
        P("exp", None, "ctx"),
        P("exp", None, "ctx"),
        P("exp", "ctx", None),
        P("ctx", None, None),
        P("ctx", None, None),
    )
    return jax.shard_map(
        on_device, mesh=mesh, in_specs=placed, out_specs=P("ctx", None, "exp"), check_vma=False
    )
```

```python
import functools
import math

import jax
import jax.numpy as jnp
from jax import lax
from jax.experimental import pallas as pl
from jax.experimental.pallas import tpu as pltpu
from jax.sharding import PartitionSpec as P

epsilon = 1e-06
f32, bf16 = jnp.float32, jnp.bfloat16
MESH = pl.DeviceIdType.MESH
VMEM_LIMIT = 48 * 1024 * 1024
SMEM = pl.BlockSpec(memory_space=pltpu.SMEM)
LOCAL = pl.BlockSpec(memory_space=pltpu.VMEM)


def factors(count):
    inner = 2 ** (count.bit_length() // 2 - (1 if count.bit_length() % 2 == 0 else 0))
    return count // inner, inner


def ends_kernel(
    length, prompts, states, step_ref, signal_ref, rate_ref, into_ref, route_ref, end_ref
):
    tile = step_ref.shape[1:]
    for b in range(prompts):

        def chunk(i, carry):
            held, total = carry
            for u in range(4):
                row = (i * 4 + u) * prompts + b
                step = step_ref[row]
                inflow = step * signal_ref[row]
                held = tuple(
                    jnp.exp2(step * rate_ref[n]) * held[n] + inflow * into_ref[row * states + n]
                    for n in range(states)
                )
                total = total + step
            return held, total

        zero = jnp.zeros(tile, f32)
        held, total = lax.fori_loop(0, length // 4, chunk, ((zero,) * states, zero))
        for n in range(states):
            end_ref[b * (states + 1) + n] = held[n]
        end_ref[b * (states + 1) + states] = total
    end_ref[prompts * (states + 1) :] = route_ref[...]


def scan_kernel(
    length, prompts, states, step_ref, signal_ref, rate_ref, into_ref, outof_ref, enter_ref, out_ref
):
    for b in range(prompts):

        def chunk(i, held):
            for u in range(4):
                row = (i * 4 + u) * prompts + b
                step = step_ref[row]
                inflow = step * signal_ref[row]
                held = tuple(
                    jnp.exp2(step * rate_ref[n]) * held[n] + inflow * into_ref[row * states + n]
                    for n in range(states)
                )
                terms = [held[n] * outof_ref[row * states + n] for n in range(states)]
                while len(terms) > 1:
                    terms = [p + q for p, q in zip(terms[::2], terms[1::2])]
                out_ref[row] = terms[0]
            return held

        lax.fori_loop(0, length // 4, chunk, tuple(enter_ref[b, n] for n in range(states)))


def act_kernel(rows_ref, gain_ref, gate_ref, up_ref, out_ref, normed):
    count, features = rows_ref.shape

    @pl.when(pl.program_id(0) == 0)
    def _():
        def norm(i, _):
            here = pl.ds(pl.multiple_of(i * 32, 32), 32)
            rows = rows_ref[here].astype(f32)
            scale = lax.rsqrt(jnp.sum(rows * rows, axis=1, keepdims=True) / features + epsilon)
            normed[here] = (rows * scale * gain_ref[...]).astype(bf16)
            return 0

        lax.fori_loop(0, count // 32, norm, 0)

    gate_part = jnp.dot(normed[...], gate_ref[0], preferred_element_type=f32)
    up_part = jnp.dot(normed[...], up_ref[0], preferred_element_type=f32)
    out_ref[...] = (gate_part / (1.0 + jnp.exp(-gate_part)) * up_part).astype(bf16)


def expert_act(rows, gain, w_gate, w_up):
    count, features = rows.shape
    hidden = w_gate.shape[2]
    tile = 256 if hidden % 256 == 0 else 128
    weights = pl.BlockSpec((1, features, tile), lambda i: (0, 0, i))
    return pl.pallas_call(
        act_kernel,
        grid=(hidden // tile,),
        out_shape=jax.ShapeDtypeStruct((count, hidden), bf16),
        in_specs=[
            pl.BlockSpec((count, features), lambda i: (0, 0)),
            pl.BlockSpec((1, features), lambda i: (0, 0)),
            weights,
            weights,
        ],
        out_specs=pl.BlockSpec((count, tile), lambda i: (0, i)),
        scratch_shapes=[pltpu.VMEM((count, features), bf16)],
        compiler_params=pltpu.CompilerParams(vmem_limit_bytes=VMEM_LIMIT),
    )(rows, gain, w_gate, w_up)


def down_kernel(act_ref, weight_ref, out_ref):
    out_ref[...] = jnp.dot(
        act_ref[...], weight_ref[0], preferred_element_type=f32
    ).astype(bf16)


def expert_down(activ, w_down):
    count, hidden = activ.shape
    features = w_down.shape[2]
    return pl.pallas_call(
        down_kernel,
        grid=(features // 512,),
        out_shape=jax.ShapeDtypeStruct((count, features), bf16),
        in_specs=[
            pl.BlockSpec((count, hidden), lambda i: (0, 0)),
            pl.BlockSpec((1, hidden, 512), lambda i: (0, 0, i)),
        ],
        out_specs=pl.BlockSpec((count, 512), lambda i: (0, i)),
        compiler_params=pltpu.CompilerParams(vmem_limit_bytes=VMEM_LIMIT),
    )(activ, w_down)


def wave(barrier, peers):
    for where in peers:
        pl.semaphore_signal(barrier, inc=1, device_id=where, device_id_type=MESH)
    pl.semaphore_wait(barrier, len(peers))


def push(src, dst, send_sem, recv_sem, where):
    copy = pltpu.make_async_remote_copy(
        src_ref=src,
        dst_ref=dst,
        send_sem=send_sem,
        recv_sem=recv_sem,
        device_id=where,
        device_id_type=MESH,
    )
    copy.start()
    return copy


def far_first(count):
    return sorted(range(1, count), key=lambda k: -min(k, count - k))


def lanes_of(index, width):
    return pl.ds(pl.multiple_of(index * width, width), width)


def sending(kernel, out_shape, dtype, scratch, ident, *operands):
    return pl.pallas_call(
        kernel,
        out_shape=jax.ShapeDtypeStruct(out_shape, dtype),
        in_specs=[LOCAL] * len(operands),
        out_specs=LOCAL,
        scratch_shapes=scratch,
        compiler_params=pltpu.CompilerParams(
            collective_id=ident, has_side_effects=True, vmem_limit_bytes=VMEM_LIMIT
        ),
    )(*operands)


def gather_ctx(x, out_shape, count, target, ident):
    chips = count // 2

    def kernel(x_ref, o_ref, send_sem, recv_sem):
        me = lax.axis_index("ctx")
        chip, core = me // 2, lax.rem(me, 2)
        twin = {"ctx": chip * 2 + (1 - core)}
        others = [{"ctx": lax.rem(chip + k, chips) * 2 + core} for k in range(1, chips)]
        wave(pltpu.get_barrier_semaphore(), [twin] + others)
        across = [
            push(x_ref, target(o_ref, me), send_sem.at[k], recv_sem.at[k], others[k - 1])
            for k in range(1, chips)
        ]
        pending = [push(x_ref, target(o_ref, me), send_sem.at[0], recv_sem.at[0], twin)]
        target(o_ref, me)[...] = x_ref[...]
        for k in range(1, chips):
            across[k - 1].wait_recv()
            view = target(o_ref, lax.rem(chip + chips - k, chips) * 2 + core)
            slot = chips - 1 + k
            pending.append(push(view, view, send_sem.at[slot], recv_sem.at[slot], twin))
        for copy in across:
            copy.wait_send()
        for copy in pending:
            copy.wait()

    slots = pltpu.SemaphoreType.DMA((2 * chips - 1,))
    return sending(kernel, out_shape, x.dtype, [slots, slots], ident, x)


def scatter_sum(x, tokens, width, halves, count, parts, ident):
    outer, inner = factors(count)
    rows = tokens // parts

    def kernel(x_ref, o_ref, got1, part, got2, send1, recv1, send2, recv2):
        me = lax.axis_index("exp")
        o_me, i_me = me // inner, lax.rem(me, inner)
        near = [{"exp": o_me * inner + lax.rem(i_me + k, inner)} for k in range(1, inner)]
        far = [{"exp": lax.rem(o_me + j, outer) * inner + i_me} for j in range(1, outer)]
        wave(pltpu.get_barrier_semaphore(), near + far)

        def view(o, i, p):
            e = o * inner + i
            first = pl.multiple_of((e // halves) * tokens + p * rows, rows)
            return x_ref.at[pl.ds(first, rows), lanes_of(lax.rem(e, halves), width)]

        order = [(j % outer, p) for j in range(1, outer + 1) for p in range(parts)]
        first, sent = {}, []
        for j, p in order:
            for k in range(1, inner):
                copy = push(
                    view(lax.rem(o_me + j, outer), lax.rem(i_me + k, inner), p),
                    got1.at[k - 1, j, p],
                    send1.at[k - 1, j, p],
                    recv1.at[k - 1, j, p],
                    near[k - 1],
                )
                first[k, j, p] = copy
                sent.append(copy)

        def near_sum(j, p):
            total = view(lax.rem(o_me + j, outer), i_me, p)[...].astype(f32)
            for k in range(1, inner):
                first[k, j, p].wait_recv()
                total = total + got1[k - 1, j, p].astype(f32)
            return total

        second = {}
        for j, p in order:
            if j == 0:
                continue
            part[j - 1, p] = near_sum(j, p).astype(bf16)
            second[j, p] = push(
                part.at[j - 1, p],
                got2.at[j - 1, p],
                send2.at[j - 1, p],
                recv2.at[j - 1, p],
                far[j - 1],
            )
            sent.append(second[j, p])
        for p in range(parts):
            total = near_sum(0, p)
            for j in range(1, outer):
                second[j, p].wait_recv()
                total = total + got2[j - 1, p].astype(f32)
            o_ref[p * rows : (p + 1) * rows] = total
        for copy in sent:
            copy.wait_send()

    sem1 = pltpu.SemaphoreType.DMA((inner - 1, outer, parts))
    sem2 = pltpu.SemaphoreType.DMA((outer - 1, parts))
    scratch = [
        pltpu.VMEM((inner - 1, outer, parts, rows, width), bf16),
        pltpu.VMEM((outer - 1, parts, rows, width), bf16),
        pltpu.VMEM((outer - 1, parts, rows, width), bf16),
        sem1, sem1, sem2, sem2,
    ]
    return sending(kernel, (tokens, width), f32, scratch, ident, x)


def dispatch(x, n_ctx, n_exp, ident):
    _, cap, width = x.shape
    halves, chips = n_exp // n_ctx, n_ctx // 2

    def kernel(x_ref, o_ref, s_in, r_in, s_twin, r_twin, s_far, r_far, s_fwd, r_fwd):
        ctx, me = lax.axis_index("ctx"), lax.axis_index("exp")
        chip, core = ctx // 2, lax.rem(ctx, 2)
        twin = {"ctx": chip * 2 + (1 - core)}
        others = [{"ctx": lax.rem(chip + k, chips) * 2 + core} for k in range(1, chips)]
        peers = [{"exp": lax.rem(me + k, n_exp)} for k in range(1, n_exp)]
        wave(pltpu.get_barrier_semaphore(), [twin] + others + peers)

        def view(c, e):
            first = pl.multiple_of((e // halves) * cap, cap)
            return o_ref.at[pl.ds(first, cap), lanes_of(c * halves + lax.rem(e, halves), width)]

        arriving = {
            k: push(
                x_ref.at[lax.rem(me + k, n_exp)], view(ctx, me),
                s_in.at[k - 1], r_in.at[k - 1], peers[k - 1],
            )
            for k in far_first(n_exp)
        }
        view(ctx, me)[...] = x_ref[me]
        turns = [0] + far_first(n_exp)[::-1]
        far, near = {}, []
        for j in turns:
            if j:
                arriving[j].wait_recv()
            mine = view(ctx, lax.rem(me + n_exp - j, n_exp))
            for k in range(1, chips):
                far[k, j] = push(
                    mine, mine, s_far.at[k - 1, j], r_far.at[k - 1, j], others[k - 1]
                )
            near.append(push(mine, mine, s_twin.at[j], r_twin.at[j], twin))
        for j in turns:
            for k in range(1, chips):
                far[k, j].wait_recv()
                owner = lax.rem(chip + chips - k, chips) * 2 + core
                theirs = view(owner, lax.rem(me + n_exp - j, n_exp))
                near.append(push(theirs, theirs, s_fwd.at[k - 1, j], r_fwd.at[k - 1, j], twin))
        for copy in [*arriving.values(), *far.values()]:
            copy.wait_send()
        for copy in near:
            copy.wait()

    sem_in = pltpu.SemaphoreType.DMA((n_exp - 1,))
    sem_twin = pltpu.SemaphoreType.DMA((n_exp,))
    sem_far = pltpu.SemaphoreType.DMA((chips - 1, n_exp))
    scratch = [sem_in, sem_in, sem_twin, sem_twin, sem_far, sem_far, sem_far, sem_far]
    return sending(kernel, (n_ctx * cap, n_exp * width), x.dtype, scratch, ident, x)


def combine(x, weight, n_ctx, n_exp, ident):
    _, cap, features = x.shape
    width, chips = features // n_exp, n_ctx // 2

    def kernel(x_ref, w_ref, o_ref, got1, part, got2, ready, s1, r1, s2, r2, s3, r3):
        ctx, me = lax.axis_index("ctx"), lax.axis_index("exp")
        chip, core = ctx // 2, lax.rem(ctx, 2)
        twin = {"ctx": chip * 2 + (1 - core)}
        others = [{"ctx": lax.rem(chip + k, chips) * 2 + core} for k in range(1, chips)]
        peers = [{"exp": lax.rem(me + k, n_exp)} for k in range(1, n_exp)]
        wave(pltpu.get_barrier_semaphore(), [twin] + others + peers)
        columns = [lanes_of(lax.rem(me + j, n_exp), width) for j in range(n_exp)]
        turns = far_first(n_exp) + [0]
        first, sent = {}, []
        for j in turns:
            for k in [*range(1, chips), 0]:
                block = lax.rem(chip + k, chips) * 2 + (1 - core)
                first[j, k] = push(
                    x_ref.at[block, :, columns[j]], got1.at[k, :, columns[j]],
                    s1.at[j, k], r1.at[j, k], twin,
                )
                sent.append(first[j, k])

        def near_sum(j, k):
            first[j, k].wait_recv()
            block = lax.rem(chip + k, chips) * 2 + core
            return x_ref[block, :, columns[j]].astype(f32) + got1[k, :, columns[j]].astype(f32)

        second = {}
        for j in turns:
            for k in range(1, chips):
                part[k - 1, :, columns[j]] = near_sum(j, k).astype(bf16)
                second[j, k] = push(
                    part.at[k - 1, :, columns[j]], got2.at[k - 1, :, columns[j]],
                    s2.at[j, k - 1], r2.at[j, k - 1], others[k - 1],
                )
                sent.append(second[j, k])
        last = []
        for j in turns:
            total = near_sum(j, 0)
            for k in range(1, chips):
                second[j, k].wait_recv()
                total = total + got2[k - 1, :, columns[j]].astype(f32)
            total = (total * w_ref[...]).astype(bf16)
            if j:
                ready[j - 1] = total
                last.append(
                    push(ready.at[j - 1], o_ref.at[me], s3.at[j - 1], r3.at[j - 1], peers[j - 1])
                )
            else:
                o_ref[me] = total
        for copy in sent:
            copy.wait_send()
        for copy in last:
            copy.wait()

    sem1 = pltpu.SemaphoreType.DMA((n_exp, chips))
    sem2 = pltpu.SemaphoreType.DMA((n_exp, chips - 1))
    sem3 = pltpu.SemaphoreType.DMA((n_exp - 1,))
    scratch = [
        pltpu.VMEM((chips, cap, features), bf16),
        pltpu.VMEM((chips - 1, cap, features), bf16),
        pltpu.VMEM((chips - 1, cap, features), bf16),
        pltpu.VMEM((n_exp - 1, cap, width), bf16),
        sem1, sem1, sem2, sem2, sem3, sem3,
    ]
    return sending(kernel, (n_exp, cap, width), bf16, scratch, ident, x, weight)


def block(ref, r):
    return ref.at[r]


def on_device(
    mixer_input,
    gate_in,
    step_size,
    decay_rate,
    state_in,
    state_out,
    skip,
    out_proj,
    hidden_in,
    norm_gain,
    w_gate,
    w_up,
    w_down,
    route_ids,
    route_weight,
):
    slab_len, prompts, channels = mixer_input.shape
    states = decay_rate.shape[0]
    tokens = slab_len * prompts
    n_ctx, n_exp = lax.axis_size("ctx"), lax.axis_size("exp")
    ctx, exp = lax.axis_index("ctx"), lax.axis_index("exp")
    share = hidden_in.shape[-1]
    halves = n_exp // n_ctx
    cap = 4 * tokens // (w_gate.shape[0] * n_exp)

    swap = [
        (c * n_exp + e, (e // halves) * n_exp + c * halves + e % halves)
        for c in range(n_ctx)
        for e in range(n_exp)
    ]
    hidden = lax.ppermute(hidden_in.reshape(tokens, share), ("ctx", "exp"), swap)
    slab = exp // halves

    def selector(routed):
        named = jnp.any(routed[:, :, None] == jnp.arange(n_exp)[None, None, :], axis=1)
        place = jnp.cumsum(named.astype(jnp.int32), axis=0) - 1
        place = jnp.where(named, place, -1).T
        return place[:, None, :] == jnp.arange(cap)[None, :, None]

    lanes = (channels // 128, 128)
    signal = mixer_input.astype(f32).reshape(tokens, *lanes)
    step = step_size.reshape(tokens, *lanes)
    rate = (decay_rate * (-1.0 / math.log(2.0))).reshape(states, *lanes)
    into, outof = state_in.reshape(-1), state_out.reshape(-1)
    plain = pltpu.CompilerParams(vmem_limit_bytes=VMEM_LIMIT)
    named = route_ids.reshape(-1).astype(f32)
    named = jnp.pad(named, (0, -named.size % channels)).reshape(-1, *lanes)
    summary = prompts * (states + 1)
    ends = pl.pallas_call(
        functools.partial(ends_kernel, slab_len, prompts, states),
        out_shape=jax.ShapeDtypeStruct((summary + named.shape[0],) + lanes, f32),
        in_specs=[LOCAL, LOCAL, LOCAL, SMEM, LOCAL],
        out_specs=LOCAL,
        compiler_params=plain,
    )(step, signal, rate, into, named)
    ends = gather_ctx(ends, (n_ctx,) + ends.shape, n_ctx, block, 1)
    routes = ends[:, summary:].reshape(n_ctx, -1)[:, : route_ids.size].astype(jnp.int32)
    routes = routes.reshape(n_ctx, tokens, -1)
    ends = ends[:, :summary].reshape((n_ctx, prompts, states + 1) + lanes)
    entering = jnp.zeros((prompts, states) + lanes, f32)
    for j in range(n_ctx - 1):
        longer = jnp.exp2(ends[j, :, states:] * rate[None]) * entering + ends[j, :, :states]
        entering = jnp.where(j < ctx, longer, entering)
    output = pl.pallas_call(
        functools.partial(scan_kernel, slab_len, prompts, states),
        out_shape=jax.ShapeDtypeStruct((tokens,) + lanes, f32),
        in_specs=[LOCAL, LOCAL, LOCAL, SMEM, SMEM, LOCAL],
        out_specs=LOCAL,
        compiler_params=plain,
    )(step, signal, rate, into, outof, entering)
    output = output.reshape(tokens, channels) + skip * mixer_input.astype(f32).reshape(tokens, -1)
    mixed = (output * jax.nn.silu(gate_in.astype(f32).reshape(tokens, -1))).astype(bf16)

    mixed = gather_ctx(
        mixed, (n_ctx * tokens, channels), n_ctx,
        lambda ref, c: ref.at[pl.ds(pl.multiple_of(c * tokens, tokens), tokens)], 2,
    )
    partial_value = jnp.dot(mixed, out_proj, preferred_element_type=f32).astype(bf16)
    projected = scatter_sum(partial_value, tokens, share, halves, n_exp, 4, 3)
    residual = hidden.astype(f32) + projected

    chosen = selector(lax.dynamic_index_in_dim(routes, slab, 0, keepdims=False))
    rows = jnp.dot(
        chosen.astype(bf16).reshape(n_exp * cap, tokens),
        residual.astype(bf16),
        preferred_element_type=f32,
    ).astype(bf16)
    rows = dispatch(rows.reshape(n_exp, cap, share), n_ctx, n_exp, 4)
    rows, residual = lax.optimization_barrier((rows, residual))
    residual_home = lax.ppermute(residual, ("ctx", "exp"), swap)
    activ = expert_act(rows, norm_gain[None, :], w_gate, w_up)
    down = expert_down(activ, w_down)

    own = selector(route_ids.reshape(tokens, -1))
    weights = route_weight.reshape(tokens, -1)
    strength = jnp.sum(jnp.where(route_ids.reshape(tokens, -1) == exp, weights, 0.0), axis=1)
    mine = lax.dynamic_index_in_dim(own, exp, 0, keepdims=False)
    slot_weight = jnp.sum(jnp.where(mine, strength[None, :], 0.0), axis=1)
    slot_weight = jnp.broadcast_to(slot_weight[:, None], (cap, share))
    back = combine(down.reshape(n_ctx, cap, -1), slot_weight, n_ctx, n_exp, 5)
    combined = lax.dot_general(
        own.astype(bf16).reshape(n_exp * cap, tokens),
        back.reshape(n_exp * cap, share),
        (((0,), (0,)), ((), ())),
        preferred_element_type=f32,
    )
    return (residual_home + combined).astype(bf16).reshape(slab_len, prompts, share)


def solution(mesh):
    placed = (
        P("ctx", None, "exp"),
        P("ctx", None, "exp"),
        P("ctx", None, "exp"),
        P(None, "exp"),
        P("ctx", None, None),
        P("ctx", None, None),
        P("exp"),
        P("exp", "ctx"),
        P("ctx", None, "exp"),
        P(),
        P("exp", None, "ctx"),
        P("exp", None, "ctx"),
        P("exp", "ctx", None),
        P("ctx", None, None),
        P("ctx", None, None),
    )
    return jax.shard_map(
        on_device, mesh=mesh, in_specs=placed, out_specs=P("ctx", None, "exp"), check_vma=False
    )
```
